256 devices in a mesh: section: 16 (over x_lo, z), dp: 16 (over x_hi, y, core).
Axes of the slice: x: 4 (x_hi: 2, x_lo: 2; x = x_hi * 2 + x_lo), y: 4, z: 8, core: 2. Of those that a mesh axis runs over, the one named last changes fastest.
Arguments:
- activations: bfloat16 [16, 64, 64, 8192], P('section', 'dp'), may hold values from -6 to 6
- out_grads: bfloat16 [16, 64, 64, 8192], P('section', 'dp'), may hold values from -6 to 6
- proj_in: bfloat16 [16, 64, 8192], P('section'), may hold values from -0.0625 to 0.0625
- proj_out: bfloat16 [16, 64, 8192], P('section'), may hold values from -0.0625 to 0.0625
- queries: bfloat16 [16, 256, 4096], P('section', 'dp'), may hold values from -6 to 6
- lengths: int32 [16, 4], P('dp'), may hold values from 1 to 64, 160 in all within a row
Outputs:
- scores: float32 [64, 256], P('dp')
The draws below stay inside these ranges and needn't reach their ends.
Inputs may be any that keep to these rules, and one draw needn't show every extreme that they name: `lengths`: the 4 examples of each data group use 5 * 32 tokens together, and one of them all 64.
All inputs are finite; a program needn't handle non-finite values.
Results may differ from the reference program's by a relative error of at most 0.005.
Values may be sent and summed in bfloat16 or wider, within the bound.
No kernel may reach another device: no remote copies, remote signals or barrier semaphores. Data moves between devices by JAX's collectives and lax.ppermute only.
A program may use at most 64 MiB of HBM per device.

```python
import math
import jax
import jax.numpy as jnp
import numpy as np
from jax import lax

D = 8192
PROJ = 64
SEQ = 64
E_DEV = 4
LAYERS = 16
EXAMPLES = 64
GROUPS = 16
NQ = 256


def level_of(stream_key, shape, shards, low, top_value):
    def one(position, blocks):
        draws = jax.random.uniform(jax.random.fold_in(jax.random.fold_in(stream_key, 6), position), (blocks,), jnp.float32, low / len(shards), top_value / len(shards))
        return jnp.repeat(jnp.exp(draws), shape[position] // blocks).reshape((-1,) + (1,) * (len(shape) - position - 1))

    factor_of = one(*shards[0])
    for cut in shards[1:]:
        factor_of = factor_of * one(*cut)
    return factor_of


def profile(count, total, most, slope):
    portions = [(1 << 20) // math.isqrt(grade ** slope) + 1 for grade in range(2, count + 1)]
    rest, holding = total - most - (count - 1), [1] * (count - 1)
    while rest > 0:
        free = [i for i in range(count - 1) if holding[i] < most]
        whole, budget = sum([portions[i] for i in free]), rest
        for i in free:
            extra = min(most - holding[i], max(1, budget * portions[i] // whole), rest)
            holding[i] = holding[i] + extra
            rest = rest - extra
    return np.array([most] + holding)


def ragged(own_key, count, total, bound, lean):
    if count == 2:
        one = jax.random.randint(own_key, (), max(1, total - bound), min(bound, total - 1) + 1)
        return jnp.stack([one, total - one])
    sizes = jnp.asarray(profile(count, total, bound, lean), jnp.int32)
    couples = (count - 1) // 2
    source_of, sink = sizes[1:1 + 2 * couples:2], sizes[2:2 + 2 * couples:2]
    margin = jnp.minimum(source_of - 1, bound - sink)
    shifted = jax.random.randint(jax.random.fold_in(own_key, 1), (couples,), 0, 1 << 20) % (margin + 1)
    sizes = sizes.at[1:1 + 2 * couples:2].set(source_of - shifted).at[2:2 + 2 * couples:2].set(sink + shifted)
    return sizes[jax.random.permutation(jax.random.fold_in(own_key, 2), count)]


def scatter_about(key, extent, spread, reach, split=(), held_as=jnp.bfloat16):
    array = jax.random.normal(key, extent, jnp.float32) * spread
    if len(split) > 0:
        array = level_of(key, extent, split, -0.22, 0.18) * array
    return jnp.clip(array, min=-reach, max=reach).astype(held_as)


def setup_inputs(seed: int = 0) -> dict:
    key_list = jax.random.split(jax.random.key(seed), 7)
    activations = scatter_about(key_list[0], (LAYERS, EXAMPLES, SEQ, D), 1.0, 6.0, ((0, 16), (1, 16)))
    out_grads = scatter_about(key_list[1], (LAYERS, EXAMPLES, SEQ, D), 1.0, 6.0, ((0, 16), (1, 16)))
    proj_in = scatter_about(key_list[2], (LAYERS, PROJ, D), D ** -0.5, 0.0625, ((0, 16),))
    proj_out = scatter_about(key_list[3], (LAYERS, PROJ, D), D ** -0.5, 0.0625, ((0, 16),))
    queries = scatter_about(key_list[4], (LAYERS, NQ, PROJ * PROJ), 1.0, 6.0, ((0, 16), (1, 16)))
    lengths = jax.vmap(lambda own: ragged(own, E_DEV, 5 * SEQ // 2, SEQ, 0))(jax.random.split(key_list[5], GROUPS)).reshape((GROUPS, E_DEV)).astype(jnp.int32)
    return {"activations": activations, "out_grads": out_grads, "proj_in": proj_in, "proj_out": proj_out, "queries": queries, "lengths": lengths}


def reference(activations, out_grads, proj_in, proj_out, queries, lengths):
    lengths_flat = lengths.reshape(-1)
    positions = jnp.arange(SEQ, dtype=jnp.int32)
    token_mask = (positions[None, :] < lengths_flat[:, None]).astype(jnp.bfloat16)

    def one_layer(running, layer_items):
        layer_acts, layer_grads, matrix_in, matrix_out, query_block = layer_items
        in_coords = jnp.dot(layer_acts.reshape(-1, D), matrix_in.T, preferred_element_type=jnp.float32)
        in_coords = in_coords.astype(jnp.bfloat16).reshape(EXAMPLES, SEQ, PROJ) * token_mask[:, :, None]
        out_coords = jnp.dot(layer_grads.reshape(-1, D), matrix_out.T, preferred_element_type=jnp.float32)
        out_coords = out_coords.astype(jnp.bfloat16).reshape(EXAMPLES, SEQ, PROJ)
        projected = jnp.einsum("esj,esk->ejk", out_coords.astype(jnp.float32), in_coords.astype(jnp.float32))
        projected = projected.astype(jnp.bfloat16).reshape(EXAMPLES, PROJ * PROJ)
        partial_scores = jnp.dot(projected, query_block.T, preferred_element_type=jnp.float32)
        return running + partial_scores, None

    start_scores = jnp.zeros((EXAMPLES, NQ), jnp.float32)
    summed_scores, unused = lax.scan(one_layer, start_scores, (activations, out_grads, proj_in, proj_out, queries))
    norm_factor = 1.0 / (PROJ * (SEQ * LAYERS) ** 0.5)
    return summed_scores * norm_factor
```

```python
import functools

import jax
import jax.numpy as jnp
from jax import lax
from jax.experimental import pallas as pl
from jax.experimental.pallas import tpu as pltpu
from jax.sharding import Mesh, PartitionSpec as P

SECTION = ("xl", "z")
GROUP = ("xh", "y", "c")


def project_kernel(lengths_ref, acts_ref, grads_ref, in_ref, out_ref, projected_ref):
    examples, slots, width = acts_ref.shape[1:]
    rank = in_ref.shape[1]
    rows = examples * slots
    contract = (((1,), (1,)), ((), ()))
    in_coords = lax.dot_general(
        acts_ref[0].reshape(rows, width), in_ref[0], contract, preferred_element_type=jnp.float32
    )
    out_coords = lax.dot_general(
        grads_ref[0].reshape(rows, width), out_ref[0], contract, preferred_element_type=jnp.float32
    )
    out_coords = out_coords.astype(jnp.bfloat16)
    slot = lax.broadcasted_iota(jnp.int32, (slots, rank), 0)
    for e in range(examples):
        block = in_coords[e * slots:(e + 1) * slots]
        block = jnp.where(slot < lengths_ref[0, e], block, 0.0).astype(jnp.bfloat16)
        projected_ref[e] = lax.dot_general(
            out_coords[e * slots:(e + 1) * slots], block, (((0,), (0,)), ((), ())),
            preferred_element_type=jnp.float32,
        ).astype(jnp.bfloat16)


def project(activations, out_grads, proj_in, proj_out, lengths):
    examples, slots, width = activations.shape[1:]
    rank = proj_in.shape[1]
    whole = pl.BlockSpec(memory_space=pltpu.VMEM)
    return pl.pallas_call(
        project_kernel,
        out_shape=jax.ShapeDtypeStruct((examples, rank, rank), jnp.bfloat16),
        in_specs=[pl.BlockSpec(memory_space=pltpu.SMEM)] + [whole] * 4,
        out_specs=whole,
        compiler_params=pltpu.CompilerParams(vmem_limit_bytes=16 * 1024 * 1024),
        cost_estimate=pl.CostEstimate(
            flops=4 * examples * slots * width * rank, bytes_accessed=10 * 1024 * 1024, transcendentals=0
        ),
        name="project",
    )(lengths, activations, out_grads, proj_in, proj_out)


def swap(x, axis):
    return lax.ppermute(x, axis, [(0, 1), (1, 0)])


def body(activations, out_grads, proj_in, proj_out, queries, lengths):
    rank = proj_in.shape[1]
    slots = activations.shape[2]
    rows_y = lax.axis_size("y")
    own = queries[0]
    with jax.named_scope("queries_y"):
        along = lax.all_to_all(jnp.broadcast_to(own[None], (rows_y,) + own.shape), "y", 0, 0, tiled=True)
    with jax.named_scope("queries_core"):
        other = swap(along, "c")
    first = lax.axis_index("c") == 0
    stored = jnp.where(first, jnp.stack([along, other], 1), jnp.stack([other, along], 1))
    stored = stored.reshape(-1, own.shape[-1])
    with jax.named_scope("project"):
        projected = project(activations, out_grads, proj_in, proj_out, lengths).reshape(-1, rank * rank)
    with jax.named_scope("projected_xh"):
        distant = swap(projected, "xh")
    low = lax.axis_index("xh") == 0
    pair = jnp.where(low, jnp.concatenate([projected, distant]), jnp.concatenate([distant, projected]))
    partial = lax.dot_general(pair, stored, (((1,), (1,)), ((), ())), preferred_element_type=jnp.float32)
    partial = partial.reshape(2, 1, projected.shape[0], stored.shape[0])
    sections = lax.axis_size(SECTION)
    spread = jnp.broadcast_to(partial, (2, sections) + partial.shape[2:]).reshape((2 * sections,) + partial.shape[2:])
    with jax.named_scope("scores_all"):
        arrived = lax.all_to_all(spread, ("xh",) + SECTION, 0, 0, tiled=True)
    arrived = arrived.reshape((2, sections) + partial.shape[2:])
    summed = arrived.sum(1)
    norm_factor = 1.0 / (rank * (slots * sections) ** 0.5)
    return jnp.concatenate([summed[0], summed[1]], axis=1) * norm_factor


def solution(mesh):
    fine = Mesh(mesh.devices.reshape(2, 8, 2, 4, 2), SECTION + GROUP)
    placed = (
        P(SECTION, GROUP, None, None),
        P(SECTION, GROUP, None, None),
        P(SECTION, None, None),
        P(SECTION, None, None),
        P(SECTION, GROUP, None),
        P(GROUP, None),
    )
    return jax.shard_map(body, mesh=fine, in_specs=placed, out_specs=P(GROUP, None), check_vma=False)
```

```python
import functools

import jax
import jax.numpy as jnp
from jax import lax
from jax.experimental import pallas as pl
from jax.experimental.pallas import tpu as pltpu
from jax.sharding import Mesh, PartitionSpec as P

SECTION = ("xl", "z")
GROUP = ("xh", "y", "c")


KEPT = 192
STEPS = 4
AHEAD = 3


def project_kernel(
    lengths_hbm, acts_ref, grads_ref, in_ref, out_ref, projected_ref,
    lengths_ref, acts_buf, grads_buf, in_buf, out_buf, token_sem, weight_sem, lengths_sem,
):
    lengths_copy = pltpu.make_async_copy(lengths_hbm, lengths_ref, lengths_sem)
    lengths_copy.start()
    examples, slots, width = acts_ref.shape[1:]
    rank = in_ref.shape[1]
    part = width // STEPS
    sides = ((acts_ref, in_ref, acts_buf, in_buf), (grads_ref, out_ref, grads_buf, out_buf))
    steps = [(side, k) for k in range(STEPS) for side in range(2)]

    def weight_copy(index):
        side, k = steps[index]
        columns = pl.ds(k * part, part)
        return pltpu.make_async_copy(
            sides[side][1].at[0, :, columns], sides[side][3].at[:, columns], weight_sem.at[index % AHEAD]
        )

    def start(index):
        side, k = steps[index]
        columns = pl.ds(k * part, part)
        if index >= AHEAD:
            weight_copy(index).start()
        for e in range(examples):
            pltpu.make_async_copy(
                sides[side][0].at[0, e, pl.ds(0, padded[e]), columns],
                sides[side][2].at[pl.ds(starts[e], padded[e]), columns],
                token_sem.at[index % AHEAD],
            ).start()

    def wait(index):
        side, k = steps[index]
        weight_copy(index).wait()
        rows = sides[side][2].at[pl.ds(0, total), pl.ds(k * part, part)]
        pltpu.make_async_copy(rows, rows, token_sem.at[index % AHEAD]).wait()

    for index in range(AHEAD):
        weight_copy(index).start()
    lengths_copy.wait()
    used = [lengths_ref[0, e] for e in range(examples)]
    padded = [pl.multiple_of((u + 15) // 16 * 16, 16) for u in used]
    starts = [0]
    for e in range(examples):
        starts.append(pl.multiple_of(starts[e] + padded[e], 16))
    total = starts[examples]
    for index in range(AHEAD):
        start(index)
    coords = [None, None]
    for index, (side, k) in enumerate(steps):
        wait(index)
        if index + AHEAD < len(steps):
            start(index + AHEAD)
        columns = slice(k * part, (k + 1) * part)
        term = lax.dot_general(
            sides[side][2][:, columns], sides[side][3][:, columns], (((1,), (1,)), ((), ())),
            preferred_element_type=jnp.float32,
        )
        coords[side] = term if k == 0 else coords[side] + term
    row = lax.broadcasted_iota(jnp.int32, (KEPT, rank), 0)
    blocks = [
        jnp.where((row >= starts[e]) & (row < starts[e] + used[e]), coords[0], 0.0).astype(jnp.bfloat16)
        for e in range(examples)
    ]
    out_coords = jnp.where(row < total, coords[1], 0.0).astype(jnp.bfloat16)
    projected = lax.dot_general(
        out_coords, jnp.concatenate(blocks, axis=1), (((0,), (0,)), ((), ())),
        preferred_element_type=jnp.float32,
    ).astype(jnp.bfloat16)
    for e in range(examples):
        projected_ref[e] = projected[:, e * rank:(e + 1) * rank]


def project(activations, out_grads, proj_in, proj_out, lengths):
    examples, slots, width = activations.shape[1:]
    rank = proj_in.shape[1]
    far = pl.BlockSpec(memory_space=pltpu.HBM)
    kept = [pltpu.with_memory_space_constraint(x, pltpu.HBM) for x in (lengths, activations, out_grads, proj_in, proj_out)]
    return pl.pallas_call(
        project_kernel,
        out_shape=pltpu.VMEM((examples, rank, rank), jnp.bfloat16),
        in_specs=[far] * 5,
        out_specs=pl.BlockSpec(memory_space=pltpu.VMEM),
        scratch_shapes=[
            pltpu.SMEM(lengths.shape, jnp.int32),
            pltpu.VMEM((KEPT, width), jnp.bfloat16),
            pltpu.VMEM((KEPT, width), jnp.bfloat16),
            pltpu.VMEM((rank, width), jnp.bfloat16),
            pltpu.VMEM((rank, width), jnp.bfloat16),
            pltpu.SemaphoreType.DMA((AHEAD,)),
            pltpu.SemaphoreType.DMA((AHEAD,)),
            pltpu.SemaphoreType.DMA,
        ],
        compiler_params=pltpu.CompilerParams(vmem_limit_bytes=16 * 1024 * 1024),
        cost_estimate=pl.CostEstimate(
            flops=4 * KEPT * width * rank, bytes_accessed=16 * 1024 * 1024, transcendentals=0
        ),
        name="project",
    )(*kept)


def swap(x, axis):
    return lax.ppermute(x, axis, [(0, 1), (1, 0)])


def body(activations, out_grads, proj_in, proj_out, queries, lengths):
    rank = proj_in.shape[1]
    slots = activations.shape[2]
    rows_y = lax.axis_size("y")
    own = queries[0]
    with jax.named_scope("queries_y"):
        me = lax.axis_index("y")
        hops = [lax.ppermute(own, "y", [(i, (i + d) % rows_y) for i in range(rows_y)]) for d in range(1, rows_y)]
        from_back = jnp.stack([own] + hops)
        along = jnp.stack([lax.dynamic_index_in_dim(from_back, lax.rem(me - i + rows_y, rows_y), 0, False) for i in range(rows_y)])
    with jax.named_scope("project"):
        projected = project(activations, out_grads, proj_in, proj_out, lengths).reshape(-1, rank * rank)
    with jax.named_scope("projected_xh"):
        distant = swap(projected, "xh")
    along = along + projected[0, 0] * 0
    with jax.named_scope("queries_core"):
        other = swap(along, "c")
    first = lax.axis_index("c") == 0
    stored = jnp.where(first, jnp.stack([along, other], 1), jnp.stack([other, along], 1))
    stored = stored.reshape(-1, own.shape[-1])
    low = lax.axis_index("xh") == 0
    pair = jnp.where(low, jnp.concatenate([projected, distant]), jnp.concatenate([distant, projected]))
    partial = lax.dot_general(pair, stored, (((1,), (1,)), ((), ())), preferred_element_type=jnp.float32)
    partial = partial.reshape(2, 1, projected.shape[0], stored.shape[0])
    sections = lax.axis_size(SECTION)
    spread = jnp.broadcast_to(partial, (2, sections) + partial.shape[2:]).reshape((2 * sections,) + partial.shape[2:])
    with jax.named_scope("scores_all"):
        arrived = lax.all_to_all(spread, ("xh",) + SECTION, 0, 0, tiled=True)
    arrived = arrived.reshape((2, sections) + partial.shape[2:])
    summed = arrived.sum(1)
    norm_factor = 1.0 / (rank * (slots * sections) ** 0.5)
    return jnp.concatenate([summed[0], summed[1]], axis=1) * norm_factor


def solution(mesh):
    fine = Mesh(mesh.devices.reshape(2, 8, 2, 4, 2), SECTION + GROUP)
    placed = (
        P(SECTION, GROUP, None, None),
        P(SECTION, GROUP, None, None),
        P(SECTION, None, None),
        P(SECTION, None, None),
        P(SECTION, GROUP, None),
        P(GROUP, None),
    )
    return jax.shard_map(body, mesh=fine, in_specs=placed, out_specs=P(GROUP, None), check_vma=False)
```

```python
import jax
import jax.numpy as jnp
from jax import lax
from jax.experimental import pallas as pl
from jax.experimental.pallas import tpu as pltpu
from jax.sharding import Mesh, PartitionSpec as P

SECTION = ("xl", "z")
GROUP = ("xh", "y", "c")
FINAL = ("xh", "xl", "z")
STEPS = 8
AHEAD = 4
ORDER = (1, 2, 3)
BOTH_LAST = (((1,), (1,)), ((), ()))
BOTH_FIRST = (((0,), (0,)), ((), ()))


def project_kernel(
    lengths_hbm, acts_ref, grads_ref, in_ref, out_ref, projected_ref,
    lengths_ref, acts_buf, grads_buf, in_buf, out_buf, sums_ref, piece_sem, lengths_sem,
):
    rank, width = in_ref.shape
    examples = projected_ref.shape[0]
    slots = acts_ref.shape[0] // examples
    part = width // STEPS
    pairs = ((in_ref, in_buf), (acts_ref, acts_buf), (out_ref, out_buf), (grads_ref, grads_buf))

    def copies(k, slot):
        columns = pl.ds(pl.multiple_of(k * part, part), part)
        return [
            pltpu.make_async_copy(source.at[:, columns], target.at[:, columns], piece_sem.at[i, slot])
            for i, (source, target) in enumerate(pairs)
        ]

    lengths_copy = pltpu.make_async_copy(lengths_hbm, lengths_ref, lengths_sem)
    lengths_copy.start()
    for k in range(AHEAD):
        for copy in copies(k, k):
            copy.start()
    sums_ref[...] = jnp.zeros_like(sums_ref)

    def step(k, carry):
        slot = lax.rem(k, AHEAD)
        for copy in copies(k, slot):
            copy.wait()

        @pl.when(k + AHEAD < STEPS)
        def _():
            for copy in copies(k + AHEAD, slot):
                copy.start()

        columns = pl.ds(pl.multiple_of(k * part, part), part)
        sums_ref[0] += lax.dot_general(
            acts_buf[:, columns], in_buf[:, columns], BOTH_LAST, preferred_element_type=jnp.float32
        )
        sums_ref[1] += lax.dot_general(
            grads_buf[:, columns], out_buf[:, columns], BOTH_LAST, preferred_element_type=jnp.float32
        )
        return carry

    lax.fori_loop(0, STEPS, step, 0)
    lengths_copy.wait()
    slot = lax.broadcasted_iota(jnp.int32, (slots, rank), 0)
    for e in range(examples):
        rows = slice(e * slots, (e + 1) * slots)
        in_coords = jnp.where(slot < lengths_ref[0, e], sums_ref[0, rows], 0.0).astype(jnp.bfloat16)
        out_coords = sums_ref[1, rows].astype(jnp.bfloat16)
        projected_ref[e] = lax.dot_general(
            out_coords, in_coords, BOTH_FIRST, preferred_element_type=jnp.float32
        ).astype(jnp.bfloat16)


def project(activations, out_grads, proj_in, proj_out, lengths):
    examples, slots, width = activations.shape[1:]
    rank = proj_in.shape[1]
    rows = examples * slots
    far = pl.BlockSpec(memory_space=pltpu.HBM)
    operands = (lengths, activations.reshape(rows, width), out_grads.reshape(rows, width), proj_in[0], proj_out[0])
    return pl.pallas_call(
        project_kernel,
        out_shape=pltpu.VMEM((examples, rank, rank), jnp.bfloat16),
        in_specs=[far] * len(operands),
        out_specs=pl.BlockSpec(memory_space=pltpu.VMEM),
        scratch_shapes=[
            pltpu.SMEM(lengths.shape, jnp.int32),
            pltpu.VMEM((rows, width), jnp.bfloat16),
            pltpu.VMEM((rows, width), jnp.bfloat16),
            pltpu.VMEM((rank, width), jnp.bfloat16),
            pltpu.VMEM((rank, width), jnp.bfloat16),
            pltpu.VMEM((2, rows, rank), jnp.float32),
            pltpu.SemaphoreType.DMA((4, AHEAD)),
            pltpu.SemaphoreType.DMA,
        ],
        compiler_params=pltpu.CompilerParams(vmem_limit_bytes=16 * 1024 * 1024),
        cost_estimate=pl.CostEstimate(
            flops=4 * rows * width * rank, bytes_accessed=16 * 1024 * 1024, transcendentals=0
        ),
        name="project",
    )(*[pltpu.with_memory_space_constraint(x, pltpu.HBM) for x in operands])


def exchange(x, axis, distance):
    return lax.ppermute(x, axis, [(i, i ^ distance) for i in range(lax.axis_size(axis))])


def body(activations, out_grads, proj_in, proj_out, queries, lengths):
    rank = proj_in.shape[1]
    slots = activations.shape[2]
    own = queries[0]
    with jax.named_scope("queries_y"):
        me = lax.axis_index("y")
        held = {0: own}
        for distance in ORDER:
            held[distance] = exchange(own, "y", distance)
    with jax.named_scope("project"):
        projected = project(activations, out_grads, proj_in, proj_out, lengths).reshape(-1, rank * rank)
    with jax.named_scope("projected_xh"):
        distant = exchange(projected, "xh", 1)
    by_distance = jnp.stack([held[d] for d in range(len(held))])
    along = jnp.stack([lax.dynamic_index_in_dim(by_distance, me ^ i, 0, False) for i in range(len(held))])
    along = along + projected[0, 0] * 0
    with jax.named_scope("queries_core"):
        other = exchange(along, "c", 1)
    first = lax.axis_index("c") == 0
    stored = jnp.where(first, jnp.stack([along, other], 1), jnp.stack([other, along], 1))
    stored = stored.reshape(-1, own.shape[-1])
    low = lax.axis_index("xh") == 0
    pair = jnp.where(low, jnp.concatenate([projected, distant]), jnp.concatenate([distant, projected]))
    partial = lax.dot_general(pair, stored, BOTH_LAST, preferred_element_type=jnp.float32)
    sections = lax.axis_size(SECTION)
    sizes = [lax.axis_size(axis) for axis in FINAL]
    at = FINAL.index("xh")
    partial = partial.reshape([2 if i == at else 1 for i in range(3)] + [projected.shape[0], -1])
    spread = jnp.broadcast_to(partial, tuple(sizes) + partial.shape[3:]).reshape((-1,) + partial.shape[3:])
    with jax.named_scope("scores_all"):
        arrived = lax.all_to_all(spread, FINAL, 0, 0, tiled=True)
    arrived = arrived.reshape(tuple(sizes) + arrived.shape[1:])
    summed = arrived.sum([i for i in range(3) if i != at])
    norm_factor = 1.0 / (rank * (slots * sections) ** 0.5)
    return jnp.concatenate([summed[0], summed[1]], axis=1) * norm_factor


def solution(mesh):
    fine = Mesh(mesh.devices.reshape(2, 8, 2, 4, 2), SECTION + GROUP)
    placed = (
        P(SECTION, GROUP, None, None),
        P(SECTION, GROUP, None, None),
        P(SECTION, None, None),
        P(SECTION, None, None),
        P(SECTION, GROUP, None),
        P(GROUP, None),
    )
    return jax.shard_map(body, mesh=fine, in_specs=placed, out_specs=P(GROUP, None), check_vma=False)
```

```python
import jax
import jax.numpy as jnp
from jax import lax
from jax.experimental import pallas as pl
from jax.experimental.pallas import tpu as pltpu
from jax.sharding import Mesh, PartitionSpec as P

SECTION = ("xl", "z")
GROUP = ("xh", "y", "c")
FINAL = ("xh", "xl", "z")
STEPS = 8
AHEAD = 4
ORDER = (1, 2, 3)
BOTH_LAST = (((1,), (1,)), ((), ()))
BOTH_FIRST = (((0,), (0,)), ((), ()))


def project_kernel(
    lengths_hbm, acts_ref, grads_ref, in_ref, out_ref, projected_ref,
    lengths_ref, acts_buf, grads_buf, in_buf, out_buf, sums_ref, piece_sem, lengths_sem,
):
    rank, width = in_ref.shape
    examples = projected_ref.shape[0]
    slots = acts_ref.shape[0] // examples
    part = width // STEPS
    pairs = ((in_ref, in_buf), (acts_ref, acts_buf), (out_ref, out_buf), (grads_ref, grads_buf))

    def copies(k, slot):
        columns = pl.ds(pl.multiple_of(k * part, part), part)
        return [
            pltpu.make_async_copy(source.at[:, columns], target.at[:, columns], piece_sem.at[i, slot])
            for i, (source, target) in enumerate(pairs)
        ]

    lengths_copy = pltpu.make_async_copy(lengths_hbm, lengths_ref, lengths_sem)
    lengths_copy.start()
    for k in range(AHEAD):
        for copy in copies(k, k):
            copy.start()
    sums_ref[...] = jnp.zeros_like(sums_ref)

    def step(k, carry):
        slot = lax.rem(k, AHEAD)
        for copy in copies(k, slot):
            copy.wait()

        @pl.when(k + AHEAD < STEPS)
        def _():
            for copy in copies(k + AHEAD, slot):
                copy.start()

        columns = pl.ds(pl.multiple_of(k * part, part), part)
        sums_ref[0] += lax.dot_general(
            acts_buf[:, columns], in_buf[:, columns], BOTH_LAST, preferred_element_type=jnp.float32
        )
        sums_ref[1] += lax.dot_general(
            grads_buf[:, columns], out_buf[:, columns], BOTH_LAST, preferred_element_type=jnp.float32
        )
        return carry

    lax.fori_loop(0, STEPS, step, 0)
    lengths_copy.wait()
    slot = lax.broadcasted_iota(jnp.int32, (slots, rank), 0)
    for e in range(examples):
        rows = slice(e * slots, (e + 1) * slots)
        in_coords = jnp.where(slot < lengths_ref[0, e], sums_ref[0, rows], 0.0).astype(jnp.bfloat16)
        out_coords = sums_ref[1, rows].astype(jnp.bfloat16)
        projected_ref[e] = lax.dot_general(
            out_coords, in_coords, BOTH_FIRST, preferred_element_type=jnp.float32
        ).astype(jnp.bfloat16)


def project(activations, out_grads, proj_in, proj_out, lengths):
    examples, slots, width = activations.shape[1:]
    rank = proj_in.shape[1]
    rows = examples * slots
    far = pl.BlockSpec(memory_space=pltpu.HBM)
    operands = (lengths, activations.reshape(rows, width), out_grads.reshape(rows, width), proj_in[0], proj_out[0])
    return pl.pallas_call(
        project_kernel,
        out_shape=pltpu.VMEM((examples, rank, rank), jnp.bfloat16),
        in_specs=[far] * len(operands),
        out_specs=pl.BlockSpec(memory_space=pltpu.VMEM),
        scratch_shapes=[
            pltpu.SMEM(lengths.shape, jnp.int32),
            pltpu.VMEM((rows, width), jnp.bfloat16),
            pltpu.VMEM((rows, width), jnp.bfloat16),
            pltpu.VMEM((rank, width), jnp.bfloat16),
            pltpu.VMEM((rank, width), jnp.bfloat16),
            pltpu.VMEM((2, rows, rank), jnp.float32),
            pltpu.SemaphoreType.DMA((4, AHEAD)),
            pltpu.SemaphoreType.DMA,
        ],
        compiler_params=pltpu.CompilerParams(vmem_limit_bytes=16 * 1024 * 1024),
        cost_estimate=pl.CostEstimate(
            flops=4 * rows * width * rank, bytes_accessed=16 * 1024 * 1024, transcendentals=0
        ),
        name="project",
    )(*[pltpu.with_memory_space_constraint(x, pltpu.HBM) for x in operands])


def exchange(x, axis, distance):
    return lax.ppermute(x, axis, [(i, i ^ distance) for i in range(lax.axis_size(axis))])


def body(activations, out_grads, proj_in, proj_out, queries, lengths):
    rank = proj_in.shape[1]
    slots = activations.shape[2]
    own = queries[0]
    with jax.named_scope("queries_y"):
        me = lax.axis_index("y")
        held = {0: own}
        for distance in ORDER:
            held[distance] = exchange(own, "y", distance)
    with jax.named_scope("project"):
        projected = project(activations, out_grads, proj_in, proj_out, lengths).reshape(-1, rank * rank)
    with jax.named_scope("projected_xh"):
        distant = exchange(projected, "xh", 1)
    by_distance = jnp.stack([held[d] for d in reversed(range(len(held)))])
    along = jnp.stack([lax.dynamic_index_in_dim(by_distance, len(held) - 1 - (me ^ i), 0, False) for i in range(len(held))])
    along = along + projected[0, 0] * 0
    with jax.named_scope("queries_core"):
        other = exchange(along, "c", 1)
    first = lax.axis_index("c") == 0
    stored = jnp.where(first, jnp.stack([along, other], 1), jnp.stack([other, along], 1))
    stored = stored.reshape(-1, own.shape[-1])
    low = lax.axis_index("xh") == 0
    pair = jnp.where(low, jnp.concatenate([projected, distant]), jnp.concatenate([distant, projected]))
    partial = lax.dot_general(pair, stored, BOTH_LAST, preferred_element_type=jnp.float32)
    sections = lax.axis_size(SECTION)
    sizes = [lax.axis_size(axis) for axis in FINAL]
    at = FINAL.index("xh")
    partial = partial.reshape([2 if i == at else 1 for i in range(3)] + [projected.shape[0], -1])
    spread = jnp.broadcast_to(partial, tuple(sizes) + partial.shape[3:]).reshape((-1,) + partial.shape[3:])
    with jax.named_scope("scores_all"):
        arrived = lax.all_to_all(spread, FINAL, 0, 0, tiled=True)
    arrived = arrived.reshape(tuple(sizes) + arrived.shape[1:])
    summed = arrived.sum([i for i in range(3) if i != at])
    norm_factor = 1.0 / (rank * (slots * sections) ** 0.5)
    return jnp.concatenate([summed[0], summed[1]], axis=1) * norm_factor


def solution(mesh):
    fine = Mesh(mesh.devices.reshape(2, 8, 2, 4, 2), SECTION + GROUP)
    placed = (
        P(SECTION, GROUP, None, None),
        P(SECTION, GROUP, None, None),
        P(SECTION, None, None),
        P(SECTION, None, None),
        P(SECTION, GROUP, None),
        P(GROUP, None),
    )
    return jax.shard_map(body, mesh=fine, in_specs=placed, out_specs=P(GROUP, None), check_vma=False)
```

```python
import jax
import jax.numpy as jnp
from jax import lax
from jax.experimental import pallas as pl
from jax.experimental.pallas import tpu as pltpu
from jax.sharding import Mesh, PartitionSpec as P

SECTION = ("xl", "z")
GROUP = ("xh", "yh", "yl", "c")
NEAR = ("xh", "yh")
FINAL = ("yl", "xl", "z")
STEPS = 8
AHEAD = 4
ORDER = (1, 2, 3)
BOTH_LAST = (((1,), (1,)), ((), ()))
BOTH_FIRST = (((0,), (0,)), ((), ()))


def project_kernel(
    lengths_hbm, acts_ref, grads_ref, in_ref, out_ref, projected_ref,
    lengths_ref, acts_buf, grads_buf, in_buf, out_buf, sums_ref, piece_sem, lengths_sem,
):
    rank, width = in_ref.shape
    examples = projected_ref.shape[0]
    slots = acts_ref.shape[0] // examples
    part = width // STEPS
    pairs = ((in_ref, in_buf), (acts_ref, acts_buf), (out_ref, out_buf), (grads_ref, grads_buf))

    def copies(k, slot):
        columns = pl.ds(pl.multiple_of(k * part, part), part)
        return [
            pltpu.make_async_copy(source.at[:, columns], target.at[:, columns], piece_sem.at[i, slot])
            for i, (source, target) in enumerate(pairs)
        ]

    lengths_copy = pltpu.make_async_copy(lengths_hbm, lengths_ref, lengths_sem)
    lengths_copy.start()
    for k in range(AHEAD):
        for copy in copies(k, k):
            copy.start()
    sums_ref[...] = jnp.zeros_like(sums_ref)

    def step(k, carry):
        slot = lax.rem(k, AHEAD)
        for copy in copies(k, slot):
            copy.wait()

        @pl.when(k + AHEAD < STEPS)
        def _():
            for copy in copies(k + AHEAD, slot):
                copy.start()

        columns = pl.ds(pl.multiple_of(k * part, part), part)
        sums_ref[0] += lax.dot_general(
            acts_buf[:, columns], in_buf[:, columns], BOTH_LAST, preferred_element_type=jnp.float32
        )
        sums_ref[1] += lax.dot_general(
            grads_buf[:, columns], out_buf[:, columns], BOTH_LAST, preferred_element_type=jnp.float32
        )
        return carry

    lax.fori_loop(0, STEPS, step, 0)
    lengths_copy.wait()
    slot = lax.broadcasted_iota(jnp.int32, (slots, rank), 0)
    for e in range(examples):
        rows = slice(e * slots, (e + 1) * slots)
        in_coords = jnp.where(slot < lengths_ref[0, e], sums_ref[0, rows], 0.0).astype(jnp.bfloat16)
        out_coords = sums_ref[1, rows].astype(jnp.bfloat16)
        projected_ref[e] = lax.dot_general(
            out_coords, in_coords, BOTH_FIRST, preferred_element_type=jnp.float32
        ).astype(jnp.bfloat16)


def project(activations, out_grads, proj_in, proj_out, lengths):
    examples, slots, width = activations.shape[1:]
    rank = proj_in.shape[1]
    rows = examples * slots
    far = pl.BlockSpec(memory_space=pltpu.HBM)
    operands = (lengths, activations.reshape(rows, width), out_grads.reshape(rows, width), proj_in[0], proj_out[0])
    return pl.pallas_call(
        project_kernel,
        out_shape=pltpu.VMEM((examples, rank, rank), jnp.bfloat16),
        in_specs=[far] * len(operands),
        out_specs=pl.BlockSpec(memory_space=pltpu.VMEM),
        scratch_shapes=[
            pltpu.SMEM(lengths.shape, jnp.int32),
            pltpu.VMEM((rows, width), jnp.bfloat16),
            pltpu.VMEM((rows, width), jnp.bfloat16),
            pltpu.VMEM((rank, width), jnp.bfloat16),
            pltpu.VMEM((rank, width), jnp.bfloat16),
            pltpu.VMEM((2, rows, rank), jnp.float32),
            pltpu.SemaphoreType.DMA((4, AHEAD)),
            pltpu.SemaphoreType.DMA,
        ],
        compiler_params=pltpu.CompilerParams(vmem_limit_bytes=16 * 1024 * 1024),
        cost_estimate=pl.CostEstimate(
            flops=4 * rows * width * rank, bytes_accessed=16 * 1024 * 1024, transcendentals=0
        ),
        name="project",
    )(*[pltpu.with_memory_space_constraint(x, pltpu.HBM) for x in operands])


def exchange(x, axis, distance):
    return lax.ppermute(x, axis, [(i, i ^ distance) for i in range(lax.axis_size(axis))])


def body(activations, out_grads, proj_in, proj_out, queries, lengths):
    rank = proj_in.shape[1]
    slots = activations.shape[2]
    own = queries[0]
    with jax.named_scope("queries_y"):
        me = lax.axis_index(NEAR)
        held = {0: own}
        for distance in ORDER:
            held[distance] = exchange(own, NEAR, distance)
    with jax.named_scope("project"):
        projected = project(activations, out_grads, proj_in, proj_out, lengths).reshape(-1, rank * rank)
    with jax.named_scope("projected_xh"):
        distant = exchange(projected, "yl", 1)
    by_distance = jnp.stack([held[d] for d in reversed(range(len(held)))])
    along = jnp.stack([lax.dynamic_index_in_dim(by_distance, len(held) - 1 - (me ^ i), 0, False) for i in range(len(held))])
    along = along + projected[0, 0] * 0
    with jax.named_scope("queries_core"):
        other = exchange(along, "c", 1)
    first = lax.axis_index("c") == 0
    stored = jnp.where(first, jnp.stack([along, other], 1), jnp.stack([other, along], 1))
    stored = stored.reshape(-1, own.shape[-1])
    low = lax.axis_index("yl") == 0
    pair = jnp.where(low, jnp.concatenate([projected, distant]), jnp.concatenate([distant, projected]))
    partial = lax.dot_general(pair, stored, BOTH_LAST, preferred_element_type=jnp.float32)
    sections = lax.axis_size(SECTION)
    sizes = [lax.axis_size(axis) for axis in FINAL]
    at = FINAL.index("yl")
    partial = partial.reshape([2 if i == at else 1 for i in range(3)] + [projected.shape[0], -1])
    spread = jnp.broadcast_to(partial, tuple(sizes) + partial.shape[3:]).reshape((-1,) + partial.shape[3:])
    with jax.named_scope("scores_all"):
        arrived = lax.all_to_all(spread, FINAL, 0, 0, tiled=True)
    arrived = arrived.reshape(tuple(sizes) + arrived.shape[1:])
    summed = arrived.sum([i for i in range(3) if i != at])
    norm_factor = 1.0 / (rank * (slots * sections) ** 0.5)
    near = lax.axis_size(NEAR)
    blocks = [half.reshape(half.shape[0], near, 1, -1) for half in (summed[0], summed[1])]
    return jnp.concatenate(blocks, axis=2).reshape(projected.shape[0], -1) * norm_factor


def solution(mesh):
    fine = Mesh(mesh.devices.reshape(2, 8, 2, 2, 2, 2), SECTION + GROUP)
    placed = (
        P(SECTION, GROUP, None, None),
        P(SECTION, GROUP, None, None),
        P(SECTION, None, None),
        P(SECTION, None, None),
        P(SECTION, GROUP, None),
        P(GROUP, None),
    )
    return jax.shard_map(body, mesh=fine, in_specs=placed, out_specs=P(GROUP, None), check_vma=False)
```

```python
import jax
import jax.numpy as jnp
from jax import lax
from jax.experimental import pallas as pl
from jax.experimental.pallas import tpu as pltpu
from jax.sharding import Mesh, PartitionSpec as P

SECTION = ("xl", "z")
GROUP = ("xh", "yh", "yl", "c")
NEAR = ("xh", "yh")
FINAL = ("yl", "xl", "z")
STEPS = 8
AHEAD = 4
ORDER = (1, 2, 3)
BOTH_LAST = (((1,), (1,)), ((), ()))
BOTH_FIRST = (((0,), (0,)), ((), ()))


def project_kernel(
    lengths_hbm, acts_ref, grads_ref, in_ref, out_ref, projected_ref,
    lengths_ref, acts_buf, grads_buf, in_buf, out_buf, sums_ref, piece_sem, lengths_sem,
):
    rank, width = in_ref.shape
    examples = projected_ref.shape[0]
    slots = acts_ref.shape[0] // examples
    part = width // STEPS
    pairs = ((in_ref, in_buf), (acts_ref, acts_buf), (out_ref, out_buf), (grads_ref, grads_buf))

    def copies(k, slot):
        columns = pl.ds(pl.multiple_of(k * part, part), part)
        return [
            pltpu.make_async_copy(source.at[:, columns], target.at[:, columns], piece_sem.at[i, slot])
            for i, (source, target) in enumerate(pairs)
        ]

    lengths_copy = pltpu.make_async_copy(lengths_hbm, lengths_ref, lengths_sem)
    lengths_copy.start()
    for k in range(AHEAD):
        for copy in copies(k, k):
            copy.start()
    sums_ref[...] = jnp.zeros_like(sums_ref)

    def step(k, carry):
        slot = lax.rem(k, AHEAD)
        for copy in copies(k, slot):
            copy.wait()

        @pl.when(k + AHEAD < STEPS)
        def _():
            for copy in copies(k + AHEAD, slot):
                copy.start()

        columns = pl.ds(pl.multiple_of(k * part, part), part)
        sums_ref[0] += lax.dot_general(
            acts_buf[:, columns], in_buf[:, columns], BOTH_LAST, preferred_element_type=jnp.float32
        )
        sums_ref[1] += lax.dot_general(
            grads_buf[:, columns], out_buf[:, columns], BOTH_LAST, preferred_element_type=jnp.float32
        )
        return carry

    lax.fori_loop(0, STEPS, step, 0)
    lengths_copy.wait()
    slot = lax.broadcasted_iota(jnp.int32, (slots, rank), 0)
    for e in range(examples):
        rows = slice(e * slots, (e + 1) * slots)
        in_coords = jnp.where(slot < lengths_ref[0, e], sums_ref[0, rows], 0.0).astype(jnp.bfloat16)
        out_coords = sums_ref[1, rows].astype(jnp.bfloat16)
        projected_ref[e] = lax.dot_general(
            out_coords, in_coords, BOTH_FIRST, preferred_element_type=jnp.float32
        ).astype(jnp.bfloat16)


def project(activations, out_grads, proj_in, proj_out, lengths):
    examples, slots, width = activations.shape[1:]
    rank = proj_in.shape[1]
    rows = examples * slots
    far = pl.BlockSpec(memory_space=pltpu.HBM)
    operands = (lengths, activations.reshape(rows, width), out_grads.reshape(rows, width), proj_in[0], proj_out[0])
    return pl.pallas_call(
        project_kernel,
        out_shape=pltpu.VMEM((examples, rank, rank), jnp.bfloat16),
        in_specs=[far] * len(operands),
        out_specs=pl.BlockSpec(memory_space=pltpu.VMEM),
        scratch_shapes=[
            pltpu.SMEM(lengths.shape, jnp.int32),
            pltpu.VMEM((rows, width), jnp.bfloat16),
            pltpu.VMEM((rows, width), jnp.bfloat16),
            pltpu.VMEM((rank, width), jnp.bfloat16),
            pltpu.VMEM((rank, width), jnp.bfloat16),
            pltpu.VMEM((2, rows, rank), jnp.float32),
            pltpu.SemaphoreType.DMA((4, AHEAD)),
            pltpu.SemaphoreType.DMA,
        ],
        compiler_params=pltpu.CompilerParams(vmem_limit_bytes=16 * 1024 * 1024),
        cost_estimate=pl.CostEstimate(
            flops=4 * rows * width * rank, bytes_accessed=16 * 1024 * 1024, transcendentals=0
        ),
        name="project",
    )(*[pltpu.with_memory_space_constraint(x, pltpu.HBM) for x in operands])


def exchange(x, axis, distance):
    return lax.ppermute(x, axis, [(i, i ^ distance) for i in range(lax.axis_size(axis))])


def body(activations, out_grads, proj_in, proj_out, queries, lengths):
    rank = proj_in.shape[1]
    slots = activations.shape[2]
    own = queries[0]
    with jax.named_scope("queries_y"):
        me = lax.axis_index(NEAR)
        held = {0: own}
        for distance in ORDER:
            held[distance] = exchange(own, NEAR, distance)
    with jax.named_scope("project"):
        projected = project(activations, out_grads, proj_in, proj_out, lengths).reshape(-1, rank * rank)
    with jax.named_scope("projected_xh"):
        distant = exchange(projected, "yl", 1)
    by_distance = jnp.stack([held[d] for d in (1, 2, 3, 0)])
    along = jnp.stack([lax.dynamic_index_in_dim(by_distance, lax.rem((me ^ i) + 3, 4), 0, False) for i in range(len(held))])
    along = along + projected[0, 0] * 0
    with jax.named_scope("queries_core"):
        other = exchange(along, "c", 1)
    first = lax.axis_index("c") == 0
    stored = jnp.where(first, jnp.stack([along, other], 1), jnp.stack([other, along], 1))
    stored = stored.reshape(-1, own.shape[-1])
    low = lax.axis_index("yl") == 0
    pair = jnp.where(low, jnp.concatenate([projected, distant]), jnp.concatenate([distant, projected]))
    partial = lax.dot_general(pair, stored, BOTH_LAST, preferred_element_type=jnp.float32)
    sections = lax.axis_size(SECTION)
    sizes = [lax.axis_size(axis) for axis in FINAL]
    at = FINAL.index("yl")
    partial = partial.reshape([2 if i == at else 1 for i in range(3)] + [projected.shape[0], -1])
    spread = jnp.broadcast_to(partial, tuple(sizes) + partial.shape[3:]).reshape((-1,) + partial.shape[3:])
    with jax.named_scope("scores_all"):
        arrived = lax.all_to_all(spread, FINAL, 0, 0, tiled=True)
    arrived = arrived.reshape(tuple(sizes) + arrived.shape[1:])
    summed = arrived.sum([i for i in range(3) if i != at])
    norm_factor = 1.0 / (rank * (slots * sections) ** 0.5)
    near = lax.axis_size(NEAR)
    blocks = [half.reshape(half.shape[0], near, 1, -1) for half in (summed[0], summed[1])]
    return jnp.concatenate(blocks, axis=2).reshape(projected.shape[0], -1) * norm_factor


def solution(mesh):
    fine = Mesh(mesh.devices.reshape(2, 8, 2, 2, 2, 2), SECTION + GROUP)
    placed = (
        P(SECTION, GROUP, None, None),
        P(SECTION, GROUP, None, None),
        P(SECTION, None, None),
        P(SECTION, None, None),
        P(SECTION, GROUP, None),
        P(GROUP, None),
    )
    return jax.shard_map(body, mesh=fine, in_specs=placed, out_specs=P(GROUP, None), check_vma=False)
```
